256 devices in a mesh: dp: 16 (over y_hi, x, core), mp: 16 (over y_lo, z).
Axes of the slice: x: 4, y: 4 (y_hi: 2, y_lo: 2; y = y_hi * 2 + y_lo), z: 8, core: 2. Of those that a mesh axis runs over, the one named last changes fastest.
Arguments:
- features: bfloat16 [65536, 12544], P('dp', 'mp'), may hold values from -0.59765625 to 0.59765625
- embedding: bfloat16 [65536, 512], P(('dp', 'mp')), may hold values from -6 to 6
- centers: float32 [2048, 512], P('mp'), may hold values from -0.5 to 0.5
- labels: int32 [65536], P(('dp', 'mp')), may hold values from 0 to 2047
- logsumexp: float32 [65536], P(('dp', 'mp')), as said below
Outputs:
- center_grad: float32 [2048, 512], P('mp')
- weight_grad: float32 [12544, 512], P('mp')
The draws below stay inside these ranges and needn't reach their ends.
Inputs may be any that keep to these rules, and one draw needn't show every extreme that they name: `logsumexp`: each entry lies within 0.5 of log(2048) + 2.
All inputs are finite; a program needn't handle non-finite values.
Results may differ from the reference program's by a relative error of at most 0.0005.
The reference program's roundings to bfloat16 on the way (of `low_centers`, `dlogits` and `embed_grad`) count: a program that leaves them out, or rounds other values in their place, can miss the bound.
Values may be sent and summed in bfloat16 or wider, within the bound.
No kernel may reach another device: no remote copies, remote signals or barrier semaphores. Data moves between devices by JAX's collectives and lax.ppermute only.
A program may use at most 64 MiB of HBM per device.

```python
import math
import jax
import jax.numpy as jnp
from jax import lax

D = 512
IN = 12544
TOK_DEV = 256
ROWS = 65536
NCLS = 2048


def draw_logsumexp(key, part):
    key = jax.random.fold_in(key, 7)
    offset = jax.random.uniform(key, (ROWS,), jnp.float32, -0.5, 0.5)
    return (math.log(NCLS) + 2.0 + offset).astype(jnp.float32)


def with_ends(values, own_key, least, high):
    longest = values.shape.index(max(values.shape))
    spots = []
    for shift in (0, 1):
        where = [jax.random.randint(jax.random.fold_in(own_key, axis), (), 0, length) for axis, length in enumerate(values.shape)]
        where[longest] = (where[longest] + shift) % values.shape[longest]
        spots.append(tuple(where))
    return values.at[spots[0]].set(least).at[spots[1]].set(high)


def block_levels(own_key, shape, split, least, high):
    def one(axis_at, shards_of):
        heights = jax.random.uniform(jax.random.fold_in(jax.random.fold_in(own_key, 6), axis_at), (shards_of,), jnp.float32, least / len(split), high / len(split))
        return jnp.repeat(jnp.exp(heights), shape[axis_at] // shards_of).reshape((-1,) + (1,) * (len(shape) - axis_at - 1))

    gain = one(*split[0])
    for cut in split[1:]:
        gain = gain * one(*cut)
    return gain


def normal_values(rng, extent, scale, most, pieces=(), kind=jnp.bfloat16):
    entries = jax.random.normal(rng, extent, jnp.float32) * scale
    if len(pieces) > 0:
        entries = block_levels(rng, extent, pieces, -0.22, 0.18) * entries
    return jnp.clip(entries, min=-most, max=most).astype(kind)


def setup_inputs(seed: int = 0) -> dict:
    splits = jax.random.split(jax.random.key(seed), 6)
    return {
        "features": normal_values(splits[0], (ROWS, IN), 0.1, 0.59765625, ((0, 16), (1, 16))),
        "embedding": normal_values(splits[1], (ROWS, D), 1.0, 6.0, ((0, 256),)),
        "centers": normal_values(splits[2], (NCLS, D), (D // 4) ** -0.5, 0.5, ((0, 16),), jnp.float32),
        "labels": with_ends(jax.random.randint(splits[3], (ROWS,), 0, NCLS), jax.random.fold_in(splits[3], 1), 0, NCLS - 1).astype(jnp.int32),
        "logsumexp": draw_logsumexp(jax.random.fold_in(splits[5], 71), 0),
    }


def reference(features, embedding, centers, labels, logsumexp):
    low_centers = centers.astype(jnp.bfloat16)
    classes = jnp.arange(NCLS, dtype=jnp.int32)
    emb_blocks = embedding.reshape(-1, TOK_DEV, D)
    lab_blocks = labels.reshape(-1, TOK_DEV)
    lse_blocks = logsumexp.reshape(-1, TOK_DEV)

    def step(accum, inputs):
        emb_rows, lab_rows, lse_rows = inputs
        logits = jnp.dot(emb_rows, low_centers.T, preferred_element_type=jnp.float32)
        onehot = (lab_rows[:, None] == classes[None, :]).astype(jnp.float32)
        dlogits = (jnp.exp(logits - lse_rows[:, None]) - onehot).astype(jnp.bfloat16)
        accum = accum + jnp.dot(dlogits.T, emb_rows, preferred_element_type=jnp.float32)
        embed_grad = jnp.dot(dlogits, low_centers, preferred_element_type=jnp.float32).astype(jnp.bfloat16)
        return accum, embed_grad

    center_grad, embed_grad = lax.scan(step, jnp.zeros((NCLS, D), jnp.float32), (emb_blocks, lab_blocks, lse_blocks))
    embed_grad = embed_grad.reshape(-1, D)
    weight_grad = jnp.dot(features.T, embed_grad, preferred_element_type=jnp.float32)
    return center_grad, weight_grad
```

```python
import functools

import jax
import jax.numpy as jnp
from jax import lax
from jax.experimental import pallas as pl
from jax.experimental.pallas import tpu as pltpu
from jax.sharding import PartitionSpec as P

BF = jnp.bfloat16
F32 = jnp.float32
NZ = 8
NX = 4
ROWS = 256
NCLS = 2048
CHUNK = 512
NT = (((1,), (1,)), ((), ()))
TN = (((0,), (0,)), ((), ()))


def along_z(array, by):
    return lax.ppermute(array, "mp", [(i, i // NZ * NZ + (i + by) % NZ) for i in range(2 * NZ)])


def across_y(array):
    return lax.ppermute(array, "mp", [(i, i ^ NZ) for i in range(2 * NZ)])


def across_core(array):
    return lax.ppermute(array, "dp", [(i, i ^ 1) for i in range(16)])


def along_x(array, by):
    return lax.ppermute(
        array, "dp", [(i, i // 8 * 8 + (i // 2 + by) % NX * 2 + i % 2) for i in range(16)]
    )


def across_y_hi(array):
    return lax.ppermute(array, "dp", [(i, i ^ 8) for i in range(16)])


def unit_kernel(n, first, units, ids, meta, centers, features, *rest):
    embeddings, rest = rest[:n], rest[n:]
    if first:
        w_out, cg_out, rows, sems = rest
    else:
        w_in, cg_in, w_out, cg_out, rows, sems = rest
    copies = [
        pltpu.make_async_copy(
            features.at[pl.ds(pl.multiple_of(units[i] * ROWS, ROWS), ROWS), :],
            rows.at[pl.ds(i * ROWS, ROWS), :],
            sems.at[i],
        )
        for i in range(n)
    ]
    for copy in copies:
        copy.start()
    e = jnp.concatenate([r[...] for r in embeddings], axis=0)
    columns = [meta[units[i]].T for i in range(n)]
    lse = jnp.concatenate([c[:, 0:1] for c in columns], axis=0)
    label = jnp.concatenate([c[:, 1:2] for c in columns], axis=0).astype(jnp.int32)
    g = None
    for k in range(NCLS // CHUNK):
        part = slice(k * CHUNK, (k + 1) * CHUNK)
        block = centers[part, :]
        logits = lax.dot_general(e, block, NT, preferred_element_type=F32)
        p = jnp.exp(logits - lse)
        d = jnp.where(label == ids[:, part], p - 1.0, p).astype(BF)
        if k == 0:
            cg = lax.dot_general(d[:, :128], e, TN, preferred_element_type=F32)
            cg_out[...] = cg if first else cg_in[...] + cg
        term = jnp.dot(d, block, preferred_element_type=F32)
        g = term if g is None else g + term
    g = g.astype(BF)
    for copy in copies:
        copy.wait()
    w = lax.dot_general(rows[...], g, TN, preferred_element_type=F32)
    w_out[...] = w if first else w_in[...] + w


def add_units(embeddings, units, ids, meta, centers, features, sums):
    n = len(embeddings)
    vmem = pl.BlockSpec(memory_space=pltpu.VMEM)
    smem = pl.BlockSpec(memory_space=pltpu.SMEM)
    operands = [units, ids, meta, centers, features, *embeddings, *sums]
    specs = [smem, vmem, vmem, vmem, pl.BlockSpec(memory_space=pl.ANY)]
    specs += [vmem] * (n + len(sums))
    width = features.shape[1]
    span = 128
    return pl.pallas_call(
        functools.partial(unit_kernel, n, not sums),
        out_shape=(
            jax.ShapeDtypeStruct((width, 512), F32),
            jax.ShapeDtypeStruct((span, 512), F32),
        ),
        in_specs=specs,
        out_specs=(vmem, vmem),
        scratch_shapes=[pltpu.VMEM((n * ROWS, width), BF), pltpu.SemaphoreType.DMA((n,))],
        input_output_aliases={len(operands) - 2: 0, len(operands) - 1: 1} if sums else {},
        compiler_params=pltpu.CompilerParams(vmem_limit_bytes=40 * 1024 * 1024),
        cost_estimate=pl.CostEstimate(
            flops=n * ROWS * (4 * NCLS * 512 + 2 * width * 512),
            bytes_accessed=n * ROWS * width * 2,
            transcendentals=n * ROWS * NCLS,
        ),
        name="add_units",
    )(*operands)


def reduced(w, cg):
    place = lax.axis_index("dp")
    core, x = place % 2, place // 2 % NX
    half, span = w.shape[0] // 2, cg.shape[0] // 2

    def rows_of(which):
        return jnp.concatenate(
            [
                lax.dynamic_slice_in_dim(w, which * half, half, 0),
                lax.dynamic_slice_in_dim(cg, which * span, span, 0),
            ],
            axis=0,
        )

    both = rows_of(core) + across_core(rows_of(1 - core))
    quarter = [
        lax.dynamic_slice_in_dim(both, (x + by) % NX * 128, 128, 1) for by in range(NX)
    ]
    mine = quarter[0]
    for by in range(1, NX):
        mine = mine + along_x(quarter[by], by)
    mine = mine + across_y_hi(mine)
    whole = jnp.zeros_like(both)
    for by in range(NX):
        piece = along_x(mine, by) if by else mine
        whole = lax.dynamic_update_slice_in_dim(whole, piece, (x - by) % NX * 128, 1)
    other = across_core(whole)
    low, high = jnp.where(core == 0, whole, other), jnp.where(core == 0, other, whole)
    return (
        jnp.concatenate([low[half:], high[half:]], axis=0),
        jnp.concatenate([low[:half], high[:half]], axis=0),
    )


def per_device(features, embedding, centers, labels, logsumexp):
    place = lax.axis_index("mp")
    row, z = place // NZ, place % NZ
    core = lax.axis_index("dp") % 2
    span = centers.shape[0]
    half = span // 2

    def unit(across, by):
        return (row ^ across) * NZ + (z + by) % NZ

    meta = jnp.concatenate(
        [
            logsumexp[None],
            labels.astype(F32)[None],
            jnp.zeros((6, ROWS), F32),
        ],
        axis=0,
    )
    meta = lax.all_gather(meta, "mp", axis=0)

    low = centers.astype(BF)
    own = lax.dynamic_slice_in_dim(low, core * half, half, 0)
    first = across_y(own)
    pair = jnp.concatenate([own, first], axis=0)
    parts, where = [first], [(1, 0)]
    up = down = pair
    for by in range(1, NZ // 2):
        up, down = along_z(up, 1), along_z(down, -1)
        parts += [up, down]
        where += [(0, -by), (1, -by), (0, by), (1, by)]
    parts += [along_z(up[:half], 1), along_z(down[half:], -1)]
    where += [(0, NZ // 2), (1, NZ // 2)]
    here = jnp.concatenate(parts, axis=0)
    there = across_core(here)
    table = jnp.concatenate([low, here, there], axis=0)
    lane = jnp.arange(half, dtype=jnp.int32)
    starts = jnp.stack([unit(*w) * span for w in where])
    ids = (starts[:, None] + lane[None, :]).reshape(-1)
    ids = jnp.concatenate(
        [
            place * span + jnp.arange(span, dtype=jnp.int32),
            ids + core * half,
            ids + (1 - core) * half,
        ]
    )[None]

    got = {(0, 0): embedding}
    got[0, -1], got[0, 1] = along_z(embedding, 1), along_z(embedding, -1)
    got[1, 0] = across_y(embedding)
    got[0, -2], got[0, 2] = along_z(got[0, -1], 1), along_z(got[0, 1], -1)
    got[1, -1] = across_y(got[0, -1])
    got[0, -3], got[0, 3] = along_z(got[0, -2], 1), along_z(got[0, 2], -1)
    got[1, 1] = across_y(got[0, 1])
    got[0, 4] = along_z(got[0, -3], 1)
    got[1, 2] = along_z(got[1, 1], -1)
    got[1, -2] = across_y(got[0, -2])
    got[1, -3] = along_z(got[1, -2], 1)
    got[1, 3] = along_z(got[1, 2], -1)
    got[1, 4] = across_y(got[0, 4])

    groups = [
        [(0, 0), (0, -1), (0, 1), (1, 0)],
        [(0, -2), (0, 2), (1, -1)],
        [(0, -3), (0, 3), (1, 1)],
        [(0, 4), (1, 2), (1, -2)],
        [(1, -3), (1, 3), (1, 4)],
    ]
    sums = ()
    for group in groups:
        units = jnp.stack([unit(*w) for w in group])
        sums = add_units([got[w] for w in group], units, ids, meta, table, features, sums)
    return reduced(*sums)


def solution(mesh):
    in_specs = (
        P("dp", "mp"),
        P(("dp", "mp"), None),
        P("mp", None),
        P(("dp", "mp")),
        P(("dp", "mp")),
    )
    out_specs = (P("mp", None), P("mp", None))
    return jax.shard_map(
        per_device, mesh=mesh, in_specs=in_specs, out_specs=out_specs, check_vma=False
    )
```

```python
import functools

import jax
import jax.numpy as jnp
from jax import lax
from jax.experimental import pallas as pl
from jax.experimental.pallas import tpu as pltpu
from jax.sharding import PartitionSpec as P

BF = jnp.bfloat16
F32 = jnp.float32
NZ = 8
NX = 4
ROWS = 256
EXTRA = 16
NT = (((1,), (1,)), ((), ()))
TN = (((0,), (0,)), ((), ()))


def along_z(array, by):
    return lax.ppermute(array, "mp", [(i, i // NZ * NZ + (i + by) % NZ) for i in range(2 * NZ)])


def across_y(array):
    return lax.ppermute(array, "mp", [(i, i ^ NZ) for i in range(2 * NZ)])


def across_core(array):
    return lax.ppermute(array, "dp", [(i, i ^ 1) for i in range(16)])


def along_x(array, by):
    return lax.ppermute(
        array, "dp", [(i, i // 8 * 8 + (i // 2 + by) % NX * 2 + i % 2) for i in range(16)]
    )


def across_y_hi(array):
    return lax.ppermute(array, "dp", [(i, i ^ 8) for i in range(16)])


def pack_kernel(embedding, lse, label, message):
    message[0:ROWS, :] = embedding[...]
    high = lse[...].astype(BF)
    rest = lse[...] - high.astype(F32)
    middle = rest.astype(BF)
    low = (rest - middle.astype(F32)).astype(BF)
    tens = label[...] // 256
    lines = jnp.concatenate(
        [a.astype(F32) for a in (high, middle, low, tens, label[...] - tens * 256)]
        + [jnp.zeros((1, ROWS), F32)] * 11,
        axis=0,
    )
    message[ROWS:, 0:ROWS] = lines.astype(BF)
    message[ROWS:, ROWS:] = jnp.zeros((EXTRA, message.shape[1] - ROWS), BF)


def pack(embedding, lse, label):
    vmem = pl.BlockSpec(memory_space=pltpu.VMEM)
    return pl.pallas_call(
        pack_kernel,
        out_shape=jax.ShapeDtypeStruct((ROWS + EXTRA, embedding.shape[1]), BF),
        in_specs=[vmem] * 3,
        out_specs=vmem,
        name="pack",
    )(embedding, lse[None], label[None])


def units_kernel(n, groups, own, partial, summed, weight, *refs):
    refs = list(refs)
    take = lambda count: [refs.pop(0) for _ in range(count)]
    messages = take(n)
    blocks = [(take(1)[0], take(count)) for count in groups]
    own_ids, low = take(2) if own else (None, None)
    g_in = take(1)[0] if partial else None
    units, features = take(2) if weight else (None, None)
    w_in, cg_in = take(2) if summed else (None, None)
    cg_out = take(1)[0] if own else None
    out = take(1)[0]
    copies = []
    if weight:
        rows, sems = take(2)
        copies = [
            pltpu.make_async_copy(
                features.at[:, pl.ds(pl.multiple_of(units[i] * ROWS, ROWS), ROWS)],
                rows.at[:, pl.ds(i * ROWS, ROWS)],
                sems.at[i],
            )
            for i in range(n)
        ]
    for copy in copies:
        copy.start()
    e = jnp.concatenate([m[0:ROWS, :] for m in messages], axis=0)
    lse, label = [], []
    for m in messages:
        c = m[ROWS:, 0:ROWS].astype(F32).T
        lse.append(c[:, 0:1] + c[:, 1:2] + c[:, 2:3])
        label.append((c[:, 3:4] * 256.0 + c[:, 4:5]).astype(jnp.int32))
    lse, label = jnp.concatenate(lse, axis=0), jnp.concatenate(label, axis=0)

    def gradient(block, ids):
        logits = lax.dot_general(e, block, NT, preferred_element_type=F32)
        p = jnp.exp(logits - lse)
        return jnp.where(label == ids, p - 1.0, p).astype(BF)

    if own:
        cg = lax.dot_general(gradient(low[...], own_ids[...]), e, TN, preferred_element_type=F32)
        cg_out[...] = cg_in[...] + cg if summed else cg
    g = g_in[...] if partial else None
    for ids, parts in blocks:
        block = jnp.concatenate([r[...] for r in parts], axis=0)
        term = jnp.dot(gradient(block, ids[...]), block, preferred_element_type=F32)
        g = term if g is None else g + term
    if not weight:
        out[...] = g
        return
    g = g.astype(BF)
    for copy in copies:
        copy.wait()
    w = jnp.dot(rows[...], g, preferred_element_type=F32)
    out[...] = w_in[...] + w if summed else w


def run_units(messages, blocks, own=None, partial=None, weight=None, sums=None):
    n = len(messages)
    vmem = pl.BlockSpec(memory_space=pltpu.VMEM)
    operands, specs = list(messages), [vmem] * n
    for ids, parts in blocks:
        operands += [ids, *parts]
        specs += [vmem] * (1 + len(parts))
    if own is not None:
        operands += own
        specs += [vmem] * 2
    if partial is not None:
        operands.append(partial)
        specs.append(vmem)
    shapes, scratch, aliases = [], [], {}
    if own is not None:
        shapes.append(jax.ShapeDtypeStruct((128, 512), F32))
    if weight is not None:
        width = weight[1].shape[0]
        operands += weight
        specs += [pl.BlockSpec(memory_space=pltpu.SMEM), pl.BlockSpec(memory_space=pltpu.HBM)]
        shapes.append(jax.ShapeDtypeStruct((width, 512), F32))
        scratch = [pltpu.VMEM((width, n * ROWS), BF), pltpu.SemaphoreType.DMA((n,))]
    else:
        shapes.append(jax.ShapeDtypeStruct((n * ROWS, 512), F32))
    if sums is not None:
        aliases = {len(operands): 1, len(operands) + 1: 0}
        operands += sums
        specs += [vmem] * 2
    count = sum(len(parts) for _, parts in blocks) * 512
    return pl.pallas_call(
        functools.partial(
            units_kernel,
            n,
            [len(parts) for _, parts in blocks],
            own is not None,
            partial is not None,
            sums is not None,
            weight is not None,
        ),
        out_shape=shapes,
        in_specs=specs,
        out_specs=[vmem] * len(shapes),
        scratch_shapes=scratch,
        input_output_aliases=aliases,
        compiler_params=pltpu.CompilerParams(vmem_limit_bytes=36 * 1024 * 1024),
        cost_estimate=pl.CostEstimate(
            flops=n * ROWS * (4 * count * 512 + (2 * 784 * 512 if weight is not None else 0)),
            bytes_accessed=n * ROWS * 784 * 2,
            transcendentals=n * ROWS * count,
        ),
        name="units",
    )(*operands)


def reduced(w, cg):
    place = lax.axis_index("dp")
    core, x = place % 2, place // 2 % NX
    half, span = w.shape[0] // 2, cg.shape[0] // 2

    def rows_of(which):
        return jnp.concatenate(
            [
                lax.dynamic_slice_in_dim(w, which * half, half, 0),
                lax.dynamic_slice_in_dim(cg, which * span, span, 0),
            ],
            axis=0,
        )

    both = rows_of(core) + across_core(rows_of(1 - core))
    quarter = [
        lax.dynamic_slice_in_dim(both, (x + by) % NX * 128, 128, 1) for by in range(NX)
    ]
    mine = quarter[0]
    for by in range(1, NX):
        mine = mine + along_x(quarter[by], by)
    mine = mine + across_y_hi(mine)
    whole = jnp.zeros_like(both)
    for by in range(NX):
        piece = along_x(mine, by) if by else mine
        whole = lax.dynamic_update_slice_in_dim(whole, piece, (x - by) % NX * 128, 1)
    other = across_core(whole)
    low, high = jnp.where(core == 0, whole, other), jnp.where(core == 0, other, whole)
    return (
        jnp.concatenate([low[half:], high[half:]], axis=0),
        jnp.concatenate([low[:half], high[:half]], axis=0),
    )


def per_device(features, embedding, centers, labels, logsumexp):
    place = lax.axis_index("mp")
    row, z = place // NZ, place % NZ
    core = lax.axis_index("dp") % 2
    span = centers.shape[0]
    half = span // 2
    across = features.T

    low = centers.astype(BF)
    mine = lax.dynamic_slice_in_dim(low, core * half, half, 0)
    lines = [[r * NZ + i for i in range(NZ)] for r in range(2)]
    near = lax.all_gather(mine, "mp", axis=0, tiled=True, axis_index_groups=lines)

    got = {(0, 0): pack(embedding, logsumexp, labels)}
    got[0, -1], got[0, 1] = along_z(got[0, 0], 1), along_z(got[0, 0], -1)
    got[1, 0] = across_y(got[0, 0])
    got[0, -2], got[0, 2] = along_z(got[0, -1], 1), along_z(got[0, 1], -1)
    got[1, -1] = across_y(got[0, -1])
    got[0, -3], got[0, 3] = along_z(got[0, -2], 1), along_z(got[0, 2], -1)
    got[1, 1] = across_y(got[0, 1])
    got[0, 4] = along_z(got[0, -3], 1)
    got[1, 2] = along_z(got[1, 1], -1)
    got[1, -2] = across_y(got[0, -2])
    got[1, -3] = along_z(got[1, -2], 1)
    got[1, 3] = along_z(got[1, 2], -1)
    got[1, 4] = across_y(got[0, 4])

    far = across_y(near)
    near_swap = across_core(near)
    far_swap = across_core(far)

    lane = jnp.arange(NZ * span, dtype=jnp.int32)
    half_of = lane // (NZ * half)
    inner = (lane // half) % NZ * span + jnp.where(half_of == 0, core, 1 - core) * half + lane % half
    near_ids = (row * (NZ * span) + inner)[None]
    far_ids = ((1 - row) * (NZ * span) + inner)[None]
    own = [(place * span + jnp.arange(span, dtype=jnp.int32))[None], low]

    def unit(w):
        return (row ^ w[0]) * NZ + (z + w[1]) % NZ

    early = [(0, 0), (0, -1), (0, 1), (1, 0), (0, -2), (0, 2), (1, -1)]
    late = [w for w in got if w not in early]
    near_block = (near_ids, [near, near_swap])
    far_block = (far_ids, [far, far_swap])
    cg, g = run_units([got[w] for w in early], [near_block], own=own)
    (weight,) = run_units(
        [got[w] for w in early],
        [far_block],
        partial=g,
        weight=[jnp.stack([unit(w) for w in early]), across],
    )
    cg, weight = run_units(
        [got[w] for w in late],
        [near_block, far_block],
        own=own,
        weight=[jnp.stack([unit(w) for w in late]), across],
        sums=[weight, cg],
    )
    return reduced(weight, cg)


def solution(mesh):
    in_specs = (
        P("dp", "mp"),
        P(("dp", "mp"), None),
        P("mp", None),
        P(("dp", "mp")),
        P(("dp", "mp")),
    )
    out_specs = (P("mp", None), P("mp", None))
    return jax.shard_map(
        per_device, mesh=mesh, in_specs=in_specs, out_specs=out_specs, check_vma=False
    )
```

```python
import functools

import jax
import jax.numpy as jnp
from jax import lax
from jax.experimental import pallas as pl
from jax.experimental.pallas import tpu as pltpu
from jax.sharding import PartitionSpec as P

BF = jnp.bfloat16
F32 = jnp.float32
NZ = 8
NX = 4
ROWS = 256
EXTRA = 16
TALL = ROWS + EXTRA
NT = (((1,), (1,)), ((), ()))
TN = (((0,), (0,)), ((), ()))


def along_z(array, by):
    return lax.ppermute(array, "mp", [(i, i // NZ * NZ + (i + by) % NZ) for i in range(2 * NZ)])


def across_y(array):
    return lax.ppermute(array, "mp", [(i, i ^ NZ) for i in range(2 * NZ)])


def across_core(array):
    return lax.ppermute(array, "dp", [(i, i ^ 1) for i in range(16)])


def along_x(array, by):
    return lax.ppermute(
        array, "dp", [(i, i // 8 * 8 + (i // 2 + by) % NX * 2 + i % 2) for i in range(16)]
    )


def across_y_hi(array):
    return lax.ppermute(array, "dp", [(i, i ^ 8) for i in range(16)])


def after(*arrays):
    return list(lax.optimization_barrier(arrays))


def pack_kernel(embedding, lse, label, message):
    message[0:ROWS, :] = embedding[...]
    high = lse[...].astype(BF)
    rest = lse[...] - high.astype(F32)
    middle = rest.astype(BF)
    low = (rest - middle.astype(F32)).astype(BF)
    tens = label[...] // 256
    lines = jnp.concatenate(
        [a.astype(F32) for a in (high, middle, low, tens, label[...] - tens * 256)]
        + [jnp.zeros((1, ROWS), F32)] * 11,
        axis=0,
    )
    message[ROWS:, 0:ROWS] = lines.astype(BF)
    message[ROWS:, ROWS:] = jnp.zeros((EXTRA, message.shape[1] - ROWS), BF)


def pack(embedding, lse, label):
    vmem = pl.BlockSpec(memory_space=pltpu.VMEM)
    return pl.pallas_call(
        pack_kernel,
        out_shape=jax.ShapeDtypeStruct((ROWS + EXTRA, embedding.shape[1]), BF),
        in_specs=[vmem] * 3,
        out_specs=vmem,
        name="pack",
    )(embedding, lse[None], label[None])


def units_kernel(n, groups, own, partial, summed, weight, *refs):
    refs = list(refs)
    take = lambda count: [refs.pop(0) for _ in range(count)]
    stacked = take(1)[0] if n < 0 else None
    n = abs(n)
    messages = [stacked.at[pl.ds(i * TALL, TALL), :] for i in range(n)] if stacked is not None else take(n)
    blocks = [(take(1)[0], take(count)) for count in groups]
    own_ids, low = take(2) if own else (None, None)
    g_in = take(1)[0] if partial else None
    units, features = take(2) if weight else (None, None)
    w_in, cg_in = take(2) if summed else (None, None)
    cg_out = take(1)[0] if own else None
    out = take(1)[0]
    copies = []
    if weight:
        rows, sems = take(2)
        copies = [
            pltpu.make_async_copy(
                features.at[:, pl.ds(pl.multiple_of(units[i] * ROWS, ROWS), ROWS)],
                rows.at[:, pl.ds(i * ROWS, ROWS)],
                sems.at[i],
            )
            for i in range(n)
        ]
    for copy in copies:
        copy.start()
    e = jnp.concatenate([m[0:ROWS, :] for m in messages], axis=0)
    lse, label = [], []
    for m in messages:
        c = m[ROWS:, 0:ROWS].astype(F32).T
        lse.append(c[:, 0:1] + c[:, 1:2] + c[:, 2:3])
        label.append((c[:, 3:4] * 256.0 + c[:, 4:5]).astype(jnp.int32))
    lse, label = jnp.concatenate(lse, axis=0), jnp.concatenate(label, axis=0)

    def gradient(block, ids):
        logits = lax.dot_general(e, block, NT, preferred_element_type=F32)
        p = jnp.exp(logits - lse)
        return jnp.where(label == ids, p - 1.0, p).astype(BF)

    if own:
        cg = lax.dot_general(gradient(low[...], own_ids[...]), e, TN, preferred_element_type=F32)
        cg_out[...] = cg_in[...] + cg if summed else cg
    g = g_in[...] if partial else None
    for ids, parts in blocks:
        block = jnp.concatenate([r[...] for r in parts], axis=0)
        term = jnp.dot(gradient(block, ids[...]), block, preferred_element_type=F32)
        g = term if g is None else g + term
    if not weight:
        out[...] = g
        return
    g = g.astype(BF)
    for copy in copies:
        copy.wait()
    w = jnp.dot(rows[...], g, preferred_element_type=F32)
    out[...] = w_in[...] + w if summed else w


def run_units(messages, blocks, own=None, partial=None, weight=None, sums=None):
    stacked = not isinstance(messages, list)
    n = messages.shape[0] // TALL if stacked else len(messages)
    vmem = pl.BlockSpec(memory_space=pltpu.VMEM)
    operands = [messages] if stacked else list(messages)
    specs = [vmem] * len(operands)
    for ids, parts in blocks:
        operands += [ids, *parts]
        specs += [vmem] * (1 + len(parts))
    if own is not None:
        operands += own
        specs += [vmem] * 2
    if partial is not None:
        operands.append(partial)
        specs.append(vmem)
    shapes, scratch, aliases = [], [], {}
    if own is not None:
        shapes.append(jax.ShapeDtypeStruct((128, 512), F32))
    if weight is not None:
        width = weight[1].shape[0]
        operands += weight
        specs += [pl.BlockSpec(memory_space=pltpu.SMEM), pl.BlockSpec(memory_space=pltpu.HBM)]
        shapes.append(jax.ShapeDtypeStruct((width, 512), F32))
        scratch = [pltpu.VMEM((width, n * ROWS), BF), pltpu.SemaphoreType.DMA((n,))]
    else:
        shapes.append(jax.ShapeDtypeStruct((n * ROWS, 512), F32))
    if sums is not None:
        aliases = {len(operands): 1, len(operands) + 1: 0}
        operands += sums
        specs += [vmem] * 2
    count = sum(ids.shape[1] for ids, _ in blocks)
    return pl.pallas_call(
        functools.partial(
            units_kernel,
            -n if stacked else n,
            [len(parts) for _, parts in blocks],
            own is not None,
            partial is not None,
            sums is not None,
            weight is not None,
        ),
        out_shape=shapes,
        in_specs=specs,
        out_specs=[vmem] * len(shapes),
        scratch_shapes=scratch,
        input_output_aliases=aliases,
        compiler_params=pltpu.CompilerParams(vmem_limit_bytes=36 * 1024 * 1024),
        cost_estimate=pl.CostEstimate(
            flops=n * ROWS * (4 * count * 512 + (2 * 784 * 512 if weight is not None else 0)),
            bytes_accessed=n * ROWS * 784 * 2,
            transcendentals=n * ROWS * count,
        ),
        name="units",
    )(*operands)


def reduced(w, cg):
    place = lax.axis_index("dp")
    core, x = place % 2, place // 2 % NX
    half, span = w.shape[0] // 2, cg.shape[0] // 2

    def rows_of(which):
        return jnp.concatenate(
            [
                lax.dynamic_slice_in_dim(w, which * half, half, 0),
                lax.dynamic_slice_in_dim(cg, which * span, span, 0),
            ],
            axis=0,
        )

    both = rows_of(core) + across_core(rows_of(1 - core))
    quarter = [
        lax.dynamic_slice_in_dim(both, (x + by) % NX * 128, 128, 1) for by in range(NX)
    ]
    mine = quarter[0]
    for by in range(1, NX):
        mine = mine + along_x(quarter[by], by)
    mine = mine + across_y_hi(mine)
    w_all, cg_all = jnp.zeros_like(w), jnp.zeros_like(cg)
    for by in range(NX):
        piece = along_x(mine, by) if by else mine
        lane = (x - by) % NX * 128
        for which, part in ((core, piece), (1 - core, across_core(piece))):
            w_all = lax.dynamic_update_slice(w_all, part[:half], (which * half, lane))
            cg_all = lax.dynamic_update_slice(cg_all, part[half:], (which * span, lane))
    return cg_all, w_all


def per_device(features, embedding, centers, labels, logsumexp):
    place = lax.axis_index("mp")
    row, z = place // NZ, place % NZ
    core = lax.axis_index("dp") % 2
    span = centers.shape[0]
    half = span // 2
    across = features.T

    def unit(w):
        return (row ^ w[0]) * NZ + (z + w[1]) % NZ

    low = centers.astype(BF)
    mine = lax.dynamic_slice_in_dim(low, core * half, half, 0)
    message = pack(embedding, logsumexp, labels)
    got = {(0, 0): message}
    first = across_y(mine)
    up = down = jnp.concatenate([mine, first], axis=0)
    parts, where = [up], [(0, 0), (1, 0)]
    got[0, -1], got[0, 1] = along_z(message, 1), along_z(message, -1)
    got[1, 0] = across_y(message)
    for by in range(1, NZ // 2):
        if by == 3:
            up, down, got[0, -1], got[0, 1], got[1, 0] = after(up, down, got[0, -1], got[0, 1], got[1, 0])
        up, down = along_z(up, 1), along_z(down, -1)
        parts += [up, down]
        where += [(0, -by), (1, -by), (0, by), (1, by)]
    parts.append(along_z(up, 1))
    where += [(0, NZ // 2), (1, NZ // 2)]
    swapped = [across_core(p) for p in parts]
    starts = jnp.stack([unit(w) for w in where])[:, None] * span
    lane = jnp.arange(half, dtype=jnp.int32)[None, :]
    blocks = [
        ((starts + c * half + lane).reshape(1, -1), part)
        for c, part in ((core, parts), (1 - core, swapped))
    ]
    own = [(place * span + jnp.arange(span, dtype=jnp.int32))[None], low]

    def add(places, sums):
        cg, weight = run_units(
            [got[w] for w in places],
            blocks,
            own=own,
            weight=[jnp.stack([unit(w) for w in places]), across],
            sums=sums,
        )
        return [weight, cg]

    def ready(places, sums):
        arrays = after(*sums, *[got[w] for w in places])
        got.update(zip(places, arrays[2:]))
        return arrays[:2]

    got[0, -2], got[0, 2] = along_z(got[0, -1], 1), along_z(got[0, 1], -1)
    got[1, -1] = across_y(got[0, -1])
    second = [(0, -2), (0, 2), (1, -1)]
    got[0, 0], *arrays = after(got[0, 0], *[got[w] for w in second])
    got.update(zip(second, arrays))
    sums = add([(0, 0), (0, -1), (0, 1), (1, 0)], None)
    got[0, -3], got[0, 3] = along_z(got[0, -2], 1), along_z(got[0, 2], -1)
    got[1, 1] = across_y(got[0, 1])
    third = [(0, -3), (0, 3), (1, 1)]
    sums = ready(third + [(0, -2)], sums)
    got[0, 4] = along_z(got[0, -3], 1)
    got[1, 2] = along_z(got[1, 1], -1)
    got[1, -2] = across_y(got[0, -2])
    sums = add(second, sums)
    fourth = [(0, 4), (1, 2), (1, -2)]
    sums = ready(fourth, sums)
    got[1, -3] = along_z(got[1, -2], 1)
    got[1, 3] = along_z(got[1, 2], -1)
    got[1, 4] = across_y(got[0, 4])
    sums = add(third, sums)
    sums = ready(fourth, sums)
    weight, cg = add(fourth + [(1, -3), (1, 3), (1, 4)], sums)
    return reduced(weight, cg)


def solution(mesh):
    in_specs = (
        P("dp", "mp"),
        P(("dp", "mp"), None),
        P("mp", None),
        P(("dp", "mp")),
        P(("dp", "mp")),
    )
    out_specs = (P("mp", None), P("mp", None))
    return jax.shard_map(
        per_device, mesh=mesh, in_specs=in_specs, out_specs=out_specs, check_vma=False
    )
```
